32 devices in a mesh: sector: 16 (over z, x, core), blk: 2 (over y).
Axes of the slice: x: 2, y: 2, z: 4, core: 2. Of those that a mesh axis runs over, the one named last changes fastest.
Arguments:
- signal: bfloat16 [4, 4096, 8192], P('blk', 'sector'), may hold values from -6 to 6
- offsets: int32 [4], P('blk'), may hold values from 0 to 4095
- fraction: float32 [4, 8192], P('blk'), may hold values from 0 to 1
- radius: float32 [256], replicated, may hold values from 0.2 to 0.9
- azimuth: float32 [256], replicated, may hold values from -3.140625 to 3.140625
Outputs:
- power: float32 [512, 256], P(('sector', 'blk'))
The draws below stay inside these ranges and needn't reach their ends.
All inputs are finite; a program needn't handle non-finite values.
Results may differ from the reference program's by a relative error of at most 0.00095.
Values may be sent and summed in bfloat16 or wider, within the bound.
A program may use at most 128 MiB of HBM per device.

```python
import math
import jax
import jax.numpy as jnp
from jax import lax

MICS = 4096
NFFT = 1024
NBIN = 512
SAMPLES = 8192
BLOCKS = 4
SEGS = 15
GRID = 256


def touch_ends(values, own_key, smallest, largest):
    longest = values.shape.index(max(values.shape))
    spots = []
    for shift in (0, 1):
        where = [jax.random.randint(jax.random.fold_in(own_key, axis), (), 0, length) for axis, length in enumerate(values.shape)]
        where[longest] = (where[longest] + shift) % values.shape[longest]
        spots.append(tuple(where))
    return values.at[spots[0]].set(smallest).at[spots[1]].set(largest)


def block_scale(stream_key, shape, cuts, least, high):
    def one(dim, parts):
        steps = jax.random.uniform(jax.random.fold_in(jax.random.fold_in(stream_key, 6), dim), (parts,), jnp.float32, least / len(cuts), high / len(cuts))
        return jnp.repeat(jnp.exp(steps), shape[dim] // parts).reshape((-1,) + (1,) * (len(shape) - dim - 1))

    level = one(*cuts[0])
    for cut in cuts[1:]:
        level = level * one(*cut)
    return level


def gaussian(stream_key, shape, deviation, bound, pieces=(), kind=jnp.bfloat16):
    drawn = jax.random.normal(stream_key, shape, jnp.float32) * deviation
    if len(pieces) > 0:
        drawn = block_scale(stream_key, shape, pieces, -0.22, 0.18) * drawn
    return jnp.clip(drawn, min=-bound, max=bound).astype(kind)


def setup_inputs(seed: int = 0) -> dict:
    streams_of = jax.random.split(jax.random.key(seed), 6)
    signal = gaussian(streams_of[0], (BLOCKS, MICS, SAMPLES), 1.0, 6.0, ((0, 2), (1, 16)))
    offsets = touch_ends(jax.random.randint(streams_of[1], (BLOCKS,), 0, MICS), jax.random.fold_in(streams_of[1], 1), 0, MICS - 1).astype(jnp.int32)
    fraction = jnp.clip(1.0 * jax.random.uniform(streams_of[2], (BLOCKS, SAMPLES), jnp.float32) ** block_scale(streams_of[2], (BLOCKS, SAMPLES), ((0, 2),), -0.2, 0.2), 0.0, 1.0)
    radius = jnp.clip(jax.random.uniform(streams_of[3], (GRID,), jnp.float32, 0.2, 0.9), 0.2, 0.9)
    azimuth = jnp.clip(jax.random.uniform(streams_of[4], (GRID,), jnp.float32, -3.140625, 3.140625), -3.140625, 3.140625)
    return {"signal": signal, "offsets": offsets, "fraction": fraction, "radius": radius, "azimuth": azimuth}


wavenumber = 2.0
height = 0.5

def fourier_table(groups):
    half_bins = NFFT // 2
    per_group = half_bins // groups
    sample = lax.iota(jnp.int32, NFFT)[:, None]
    column = lax.iota(jnp.int32, 2 * half_bins)[None, :]
    group = column // (2 * per_group)
    part = column // per_group % 2
    inner = column % per_group
    frequency = group * per_group + inner
    turns = (sample * frequency % NFFT).astype(jnp.float32)
    angle = turns * (2.0 * math.pi / NFFT)
    window = 0.5 - 0.5 * jnp.cos(sample.astype(jnp.float32) * (2.0 * math.pi / NFFT))
    value = jnp.where(part == 0, jnp.cos(angle), -jnp.sin(angle))
    return (value * window / math.sqrt(3.0 * NFFT / 8.0)).astype(jnp.bfloat16)

def distances(radius, azimuth, total_mics):
    turn = lax.iota(jnp.int32, total_mics).astype(jnp.float32) * (2.0 * math.pi / total_mics)
    cycle_cos = jnp.cos(turn)[:, None]
    cycle_sin = jnp.sin(turn)[:, None]
    across = (radius * jnp.cos(azimuth))[None, :]
    along = (radius * jnp.sin(azimuth))[None, :]
    squared = 1.0 + height * height + (radius * radius)[None, :] - 2.0 * (cycle_cos * across + cycle_sin * along)
    return jnp.sqrt(squared)

def steering(frequency, distance):
    phase = wavenumber * frequency.astype(jnp.float32) * distance
    return jnp.concatenate([jnp.cos(phase), jnp.sin(phase)], 1).astype(jnp.bfloat16)

def reference(signal, offsets, fraction, radius, azimuth):
    table = fourier_table(1).astype(jnp.float32)
    half = NFFT // 2

    def one_block(inputs):
        rows_in, start, weight = inputs
        doubled = jnp.concatenate([rows_in, rows_in], 0)
        window_rows = lax.dynamic_slice_in_dim(doubled, start.astype(jnp.int32), MICS + 1, 0).astype(jnp.float32)
        mixed = (1.0 - weight[None, :]) * window_rows[:-1] + weight[None, :] * window_rows[1:]
        virtual = lax.optimization_barrier(mixed.astype(jnp.bfloat16)).astype(jnp.float32)
        halves = virtual.reshape(MICS, SAMPLES // half, half)
        upper = jnp.einsum('mhn,nc->hcm', halves[:, :-1], table[:half], precision=lax.Precision.HIGHEST)
        lower = jnp.einsum('mhn,nc->hcm', halves[:, 1:], table[half:], precision=lax.Precision.HIGHEST)
        return (upper + lower).astype(jnp.bfloat16)
    spectra = lax.map(one_block, (signal, offsets, fraction))
    distance = distances(radius, azimuth, MICS)
    snapshot_count = BLOCKS * SEGS
    flat = spectra.reshape(snapshot_count, 2 * NBIN, MICS)

    def one_bin(frequency):
        real_part = lax.dynamic_index_in_dim(flat, frequency, 1, keepdims=False).astype(jnp.float32)
        imag_part = lax.dynamic_index_in_dim(flat, frequency + NBIN, 1, keepdims=False).astype(jnp.float32)
        steer = steering(frequency, distance).astype(jnp.float32)
        from_real = jnp.dot(real_part, steer, precision=lax.Precision.HIGHEST)
        from_imag = jnp.dot(imag_part, steer, precision=lax.Precision.HIGHEST)
        along = from_real[:, :GRID] + from_imag[:, GRID:]
        across = from_imag[:, :GRID] - from_real[:, GRID:]
        return lax.optimization_barrier(jnp.sum(along * along + across * across, 0)) / (MICS * snapshot_count)
    return lax.map(one_bin, jnp.arange(NBIN, dtype=jnp.int32))
```

```python
import functools
import math

import jax
import jax.numpy as jnp
from jax import lax
from jax.experimental import pallas as pl
from jax.experimental.pallas import tpu as pltpu
from jax.sharding import PartitionSpec as P

NFFT = 1024
HALF = NFFT // 2
PARTS = 4
ROWS = 16

wavenumber = 2.0
height = 0.5


def fourier_table():
    fine_count = 32
    coarse_count = HALF // fine_count
    sample = lax.iota(jnp.int32, NFFT)
    unit = 2.0 * math.pi / NFFT

    def turns(frequency):
        angle = (frequency[:, None] * sample[None, :] % NFFT).astype(jnp.float32) * unit
        return lax.optimization_barrier((jnp.cos(angle), jnp.sin(angle)))

    coarse_cos, coarse_sin = turns(lax.iota(jnp.int32, coarse_count) * fine_count)
    fine_cos, fine_sin = turns(lax.iota(jnp.int32, fine_count))
    window = 0.5 - 0.5 * jnp.cos(sample.astype(jnp.float32) * unit)
    window = lax.optimization_barrier(window)
    coarse_cos, coarse_sin = coarse_cos[:, None, None, :], coarse_sin[:, None, None, :]
    fine_cos, fine_sin = fine_cos[None, :, None, :], fine_sin[None, :, None, :]
    part = lax.broadcasted_iota(jnp.int32, (1, 1, 2, 1), 2)
    real = coarse_cos * fine_cos - coarse_sin * fine_sin
    imag = -(coarse_sin * fine_cos + coarse_cos * fine_sin)
    value = jnp.where(part == 0, real, imag)
    table = (value * window / math.sqrt(3.0 * NFFT / 8.0)).astype(jnp.bfloat16)
    return table.reshape(2 * HALF, NFFT)


def distances(index, radius, azimuth, total_mics):
    turn = index.astype(jnp.float32) * (2.0 * math.pi / total_mics)
    cycle_cos = jnp.cos(turn)[..., None]
    cycle_sin = jnp.sin(turn)[..., None]
    across = (radius * jnp.cos(azimuth))[None, None, :]
    along = (radius * jnp.sin(azimuth))[None, None, :]
    squared = (
        1.0
        + height * height
        + (radius * radius)[None, None, :]
        - 2.0 * (cycle_cos * across + cycle_sin * along)
    )
    return jnp.sqrt(squared)


def spectra_kernel(segments, virtual_ref, table_ref, out_ref, spread):
    columns = table_ref.shape[0]
    halves, _, lanes = spread.shape
    mics = halves * lanes

    @pl.loop(0, segments)
    def _(segment):
        start = pl.multiple_of(segment * HALF, HALF)
        piece = virtual_ref[0, :, pl.ds(start, NFFT)]
        product = lax.dot_general(
            table_ref[...], piece, (((1,), (1,)), ((), ())), preferred_element_type=jnp.float32
        )
        for half in range(halves):
            spread[half, pl.ds(segment, columns, stride=ROWS), :] = product[
                :, half * lanes : (half + 1) * lanes
            ]

    for half in range(halves):
        for pad in range(segments, ROWS):
            spread[half, pl.ds(pad, columns, stride=ROWS), :] = jnp.zeros(
                (columns, lanes), jnp.float32
            )
        out_ref[0, :, half * lanes : (half + 1) * lanes] = spread[half].astype(jnp.bfloat16)


def spectra_of(virtual, table):
    blocks, mics, length = virtual.shape
    segments = length // HALF - 1
    tile = HALF
    lanes = min(mics, 128)
    return pl.pallas_call(
        functools.partial(spectra_kernel, segments),
        grid=(blocks, 2 * HALF // tile),
        in_specs=[
            pl.BlockSpec((1, mics, length), lambda b, c: (b, 0, 0)),
            pl.BlockSpec((tile, NFFT), lambda b, c: (c, 0)),
        ],
        out_specs=pl.BlockSpec((1, tile * ROWS, mics), lambda b, c: (b, c, 0)),
        out_shape=jax.ShapeDtypeStruct((blocks, 2 * HALF * ROWS, mics), jnp.bfloat16),
        scratch_shapes=[pltpu.VMEM((mics // lanes, tile * ROWS, lanes), jnp.float32)],
        compiler_params=pltpu.CompilerParams(vmem_limit_bytes=50 << 20),
        name="welch",
    )(virtual, table)


def beam_kernel(spectra_ref, one_ref, step_ref, first_ref, out_ref, now, steer):
    _, mics, points = one_ref.shape[1:]
    bins = spectra_ref.shape[3]

    @pl.when(pl.program_id(1) == 0)
    def _():
        now[...] = first_ref[0]

    @pl.loop(0, mics // ROWS)
    def _(tile):
        rows = pl.ds(pl.multiple_of(tile * ROWS, ROWS), ROWS)
        cos0, sin0 = now[0, rows], now[1, rows]
        cos1, sin1 = one_ref[0, 0, rows], one_ref[0, 1, rows]
        next_cos = cos0 * cos1 - sin0 * sin1
        next_sin = sin0 * cos1 + cos0 * sin1
        double = cos1 + cos1
        step_cos, step_sin = step_ref[0, 0, rows], step_ref[0, 1, rows]
        now[0, rows] = cos0 * step_cos - sin0 * step_sin
        now[1, rows] = sin0 * step_cos + cos0 * step_sin
        for place in range(bins):
            steer[place, 0, rows] = cos0.astype(jnp.bfloat16)
            steer[place, 1, rows] = sin0.astype(jnp.bfloat16)
            cos0, next_cos = next_cos, double * next_cos - cos0
            sin0, next_sin = next_sin, double * next_sin - sin0

    for place in range(bins):
        rows = spectra_ref[0, 0, 0, place]
        turned = jnp.concatenate([rows[ROWS:], -rows[:ROWS]], 0)
        product = jnp.dot(rows, steer[place, 0], preferred_element_type=jnp.float32)
        product += jnp.dot(turned, steer[place, 1], preferred_element_type=jnp.float32)
        out_ref[0, place] = product.astype(jnp.bfloat16)


def beams(spectra, one, step, first, part):
    blocks, groups, _, bins, rows, mics = spectra.shape
    points = one.shape[-1]
    wave = pl.BlockSpec((1, 2, mics, points), lambda b, o: (b, 0, 0, 0))
    return pl.pallas_call(
        beam_kernel,
        grid=(blocks, groups),
        in_specs=[
            pl.BlockSpec((1, 1, 1, bins, rows, mics), lambda b, o: (b, o, part, 0, 0, 0)),
            wave,
            wave,
            wave,
        ],
        out_specs=pl.BlockSpec((1, bins, rows, points), lambda b, o: (o, 0, b, 0)),
        out_shape=jax.ShapeDtypeStruct((groups, bins, blocks * rows, points), jnp.bfloat16),
        scratch_shapes=[
            pltpu.VMEM((2, mics, points), jnp.float32),
            pltpu.VMEM((bins, 2, mics, points), jnp.bfloat16),
        ],
        compiler_params=pltpu.CompilerParams(vmem_limit_bytes=40 << 20),
        cost_estimate=pl.CostEstimate(
            flops=4 * blocks * groups * bins * rows * mics * points * 4,
            bytes_accessed=blocks * groups * bins * rows * (mics + points) * 2,
            transcendentals=0,
        ),
        name="beams",
    )(spectra, one, step, first)


def add(a, b):
    return (a.astype(jnp.float32) + b.astype(jnp.float32)).astype(jnp.bfloat16)


def fold_pair(x, bit):
    sectors = lax.axis_size("sector")
    mine = lax.axis_index("sector") // bit % 2
    halves = x.reshape((x.shape[0] // 2, 2) + x.shape[1:])
    sent = lax.dynamic_index_in_dim(halves, 1 - mine, 1, keepdims=False)
    kept = lax.dynamic_index_in_dim(halves, mine, 1, keepdims=False)
    got = lax.ppermute(sent, "sector", [(i, i ^ bit) for i in range(sectors)])
    return add(kept, got)


def fold_line(x, stride):
    length = x.shape[0]
    place = lax.axis_index("sector") // stride

    def entry(i):
        return lax.dynamic_index_in_dim(x, jnp.clip(i, 0, length - 1), 0, keepdims=False)

    right = left = None
    for step in range(1, length):
        send_right = entry(length - step + place)
        send_left = entry(place + step - length)
        if right is not None:
            send_right, send_left = add(send_right, right), add(send_left, left)
        movers = [i for i in range(length - 1) if i < step]
        pairs = [(i * stride + j, (i + 1) * stride + j) for i in movers for j in range(stride)]
        last = stride * length - 1
        right = lax.ppermute(send_right, "sector", pairs)
        left = lax.ppermute(send_left, "sector", [(last - a, last - b) for a, b in pairs])
    total = entry(place).astype(jnp.float32)
    for got in (right, left):
        if got is not None:
            total = total + got.astype(jnp.float32)
    return total


def fold(x):
    sectors = lax.axis_size("sector")
    stride = 1
    while stride < 4 and sectors // stride % 2 == 0:
        x = fold_pair(x, stride)
        stride *= 2
    return fold_line(x, stride)


def local(signal, offsets, fraction, radius, azimuth):
    blocks, mics, length = signal.shape
    sectors = lax.axis_size("sector")
    sector = lax.axis_index("sector")
    total_mics = mics * sectors
    segments = length // HALF - 1
    edge = lax.ppermute(
        signal[:, :1, :], "sector", [(i, (i - 1) % sectors) for i in range(sectors)]
    )
    upper = jnp.concatenate([signal[:, 1:], edge], 1).astype(jnp.float32)
    weight = fraction[:, None, :]
    virtual = ((1.0 - weight) * signal.astype(jnp.float32) + weight * upper).astype(jnp.bfloat16)
    spectra = spectra_of(virtual, fourier_table())

    band = HALF // sectors
    bins = band // PARTS
    spectra = spectra.reshape(blocks, sectors, PARTS, bins, 2 * ROWS, mics)
    index = (sector * mics + lax.iota(jnp.int32, mics)[None, :] - offsets[:, None]) % total_mics
    distance = lax.optimization_barrier(distances(index, radius, azimuth, total_mics))

    def wave(frequency):
        phase = wavenumber * frequency * distance
        return jnp.stack([jnp.cos(phase), jnp.sin(phase)], 1)

    one, step = wave(1.0), wave(float(band))
    powers = []
    for part in range(PARTS):
        partial = beams(spectra, one, step, wave(float(part * bins)), part)
        total = fold(partial)
        powers.append(jnp.sum(total * total, 1))
    scale = 1.0 / (total_mics * blocks * segments * lax.axis_size("blk"))
    power = jnp.concatenate(powers, 0) * scale
    return lax.psum_scatter(power, "blk", scatter_dimension=0, tiled=True)


def solution(mesh):
    return jax.shard_map(
        local,
        mesh=mesh,
        in_specs=(P("blk", "sector", None), P("blk"), P("blk", None), P(), P()),
        out_specs=P(("sector", "blk"), None),
        check_vma=False,
    )
```

```python
import functools
import math

import jax
import jax.numpy as jnp
from jax import lax
from jax.experimental import pallas as pl
from jax.experimental.pallas import tpu as pltpu
from jax.sharding import PartitionSpec as P

NFFT = 1024
HALF = NFFT // 2
PARTS = 4
ROWS = 16

wavenumber = 2.0
height = 0.5


def cos_of_turns(count):
    quarter = NFFT // 4
    quadrant = (count + quarter // 2) // quarter
    angle = (count - quadrant * quarter).astype(jnp.float32) * (2.0 * math.pi / NFFT)
    square = angle * angle
    sine = 1.0 / math.factorial(9)
    cosine = 1.0 / math.factorial(8) - square * (1.0 / math.factorial(10))
    cosine = 1.0 + square * (
        -1.0 / 2 + square * (1.0 / 24 + square * (-1.0 / 720 + square * cosine))
    )
    sine = angle * (
        1.0
        + square * (-1.0 / 6 + square * (1.0 / 120 + square * (-1.0 / 5040 + square * sine)))
    )
    value = jnp.where(quadrant % 2 == 0, cosine, sine)
    turned = quadrant % 4
    return jnp.where((turned == 1) | (turned == 2), -value, value)


def fourier_table():
    row = lax.broadcasted_iota(jnp.int32, (2 * HALF, NFFT), 0)
    sample = lax.broadcasted_iota(jnp.int32, (2 * HALF, NFFT), 1)
    turns = (row // 2 * sample + row % 2 * (NFFT // 4)) % NFFT
    window = 0.5 - 0.5 * cos_of_turns(lax.broadcasted_iota(jnp.int32, (1, NFFT), 1))
    value = cos_of_turns(turns) * window
    return (value / math.sqrt(3.0 * NFFT / 8.0)).astype(jnp.bfloat16)


def distances(index, radius, azimuth, total_mics):
    turn = index.astype(jnp.float32) * (2.0 * math.pi / total_mics)
    cycle_cos = jnp.cos(turn)[..., None]
    cycle_sin = jnp.sin(turn)[..., None]
    across = (radius * jnp.cos(azimuth))[None, None, :]
    along = (radius * jnp.sin(azimuth))[None, None, :]
    squared = (
        1.0
        + height * height
        + (radius * radius)[None, None, :]
        - 2.0 * (cycle_cos * across + cycle_sin * along)
    )
    return jnp.sqrt(squared)


def spectra_kernel(segments, signal_ref, edge_ref, weight_ref, table_ref, out_ref, virtual, spread):
    columns = table_ref.shape[0]
    halves, _, lanes = spread.shape
    mics, length = signal_ref.shape[1:]
    chunk = min(256, HALF)

    @pl.when(pl.program_id(1) == 0)
    def _():
        @pl.loop(0, length // chunk)
        def _(place):
            where = pl.ds(pl.multiple_of(place * chunk, chunk), chunk)
            lower = signal_ref[0, :, where].astype(jnp.float32)
            edge = edge_ref[0, :, where].astype(jnp.float32)
            weight = weight_ref[0, :, where]
            row = lax.broadcasted_iota(jnp.int32, lower.shape, 0)
            upper = jnp.where(row == mics - 1, edge, pltpu.roll(lower, mics - 1, 0))
            mixed = (1.0 - weight) * lower + weight * upper
            virtual[where, :] = mixed.T.astype(jnp.bfloat16)

    @pl.loop(0, segments)
    def _(segment):
        start = pl.multiple_of(segment * HALF, HALF)
        product = jnp.dot(
            table_ref[...], virtual[pl.ds(start, NFFT), :], preferred_element_type=jnp.float32
        )
        for half in range(halves):
            spread[half, pl.ds(segment, columns, stride=ROWS), :] = product[
                :, half * lanes : (half + 1) * lanes
            ]

    for half in range(halves):
        for pad in range(segments, ROWS):
            spread[half, pl.ds(pad, columns, stride=ROWS), :] = jnp.zeros(
                (columns, lanes), jnp.float32
            )
        out_ref[0, :, half * lanes : (half + 1) * lanes] = spread[half].astype(jnp.bfloat16)


def spectra_of(signal, edge, weight, table):
    blocks, mics, length = signal.shape
    segments = length // HALF - 1
    tile = HALF
    lanes = min(mics, 128)
    return pl.pallas_call(
        functools.partial(spectra_kernel, segments),
        grid=(blocks, 2 * HALF // tile),
        in_specs=[
            pl.BlockSpec((1, mics, length), lambda b, c: (b, 0, 0)),
            pl.BlockSpec((1, 1, length), lambda b, c: (b, 0, 0)),
            pl.BlockSpec((1, 1, length), lambda b, c: (b, 0, 0)),
            pl.BlockSpec((tile, NFFT), lambda b, c: (c, 0)),
        ],
        out_specs=pl.BlockSpec((1, tile * ROWS, mics), lambda b, c: (b, c, 0)),
        out_shape=jax.ShapeDtypeStruct((blocks, 2 * HALF * ROWS, mics), jnp.bfloat16),
        scratch_shapes=[
            pltpu.VMEM((length, mics), jnp.bfloat16),
            pltpu.VMEM((mics // lanes, tile * ROWS, lanes), jnp.float32),
        ],
        compiler_params=pltpu.CompilerParams(vmem_limit_bytes=50 << 20),
        name="welch",
    )(signal, edge, weight, table)


def beam_kernel(*refs):
    spectra_ref, one_cos, one_sin, step_cos, step_sin, *firsts = refs[:-4]
    out_ref, now, even, odd = refs[-4:]
    blocks, groups, _, bins = spectra_ref.shape[:4]
    mics = one_cos.shape[1]
    units = blocks * groups

    def generate(unit, steer):
        block = unit // groups
        for tile in range(mics // ROWS):
            rows = pl.ds(tile * ROWS, ROWS)
            cos0, sin0 = now[0, rows], now[1, rows]
            cos1, sin1 = one_cos[block, rows], one_sin[block, rows]
            next_cos = cos0 * cos1 - sin0 * sin1
            next_sin = sin0 * cos1 + cos0 * sin1
            double = cos1 + cos1
            turn_cos, turn_sin = step_cos[block, rows], step_sin[block, rows]
            now[0, rows] = cos0 * turn_cos - sin0 * turn_sin
            now[1, rows] = sin0 * turn_cos + cos0 * turn_sin
            for place in range(bins):
                steer[place, 0, rows] = cos0.astype(jnp.bfloat16)
                steer[place, 1, rows] = sin0.astype(jnp.bfloat16)
                cos0, next_cos = next_cos, double * next_cos - cos0
                sin0, next_sin = next_sin, double * next_sin - sin0

    def multiply(unit, steer):
        block, group = unit // groups, unit % groups
        for place in range(bins):
            rows = spectra_ref[block, group, 0, place]
            turned = jnp.concatenate([rows[ROWS:], -rows[:ROWS]], 0)
            product = jnp.dot(rows, steer[place, 0], preferred_element_type=jnp.float32)
            product += jnp.dot(turned, steer[place, 1], preferred_element_type=jnp.float32)
            out_ref[group, place, block] = product.astype(jnp.bfloat16)

    @pl.loop(0, units // 2)
    def _(pair):
        @pl.when(2 * pair % groups == 0)
        def _():
            if firsts:
                now[0] = firsts[0][2 * pair // groups]
                now[1] = firsts[1][2 * pair // groups]
            else:
                now[0] = jnp.ones(now.shape[1:], jnp.float32)
                now[1] = jnp.zeros(now.shape[1:], jnp.float32)

        multiply(jnp.maximum(2 * pair - 1, 0), odd)
        generate(2 * pair, even)
        multiply(2 * pair, even)
        generate(2 * pair + 1, odd)

    multiply(units - 1, odd)


def beams(spectra, waves, part):
    blocks, groups, _, bins, rows, mics = spectra.shape
    points = waves[0].shape[-1]
    wave = pl.BlockSpec((blocks, mics, points), lambda i: (0, 0, 0))
    out = pl.pallas_call(
        beam_kernel,
        grid=(1,),
        in_specs=[
            pl.BlockSpec((blocks, groups, 1, bins, rows, mics), lambda i: (0, 0, part, 0, 0, 0))
        ]
        + [wave] * len(waves),
        out_specs=pl.BlockSpec((groups, bins, blocks, rows, points), lambda i: (0, 0, 0, 0, 0)),
        out_shape=jax.ShapeDtypeStruct((groups, bins, blocks, rows, points), jnp.bfloat16),
        scratch_shapes=[
            pltpu.VMEM((2, mics, points), jnp.float32),
            pltpu.VMEM((bins, 2, mics, points), jnp.bfloat16),
            pltpu.VMEM((bins, 2, mics, points), jnp.bfloat16),
        ],
        compiler_params=pltpu.CompilerParams(vmem_limit_bytes=48 << 20),
        cost_estimate=pl.CostEstimate(
            flops=32 * blocks * groups * bins * rows * mics * points,
            bytes_accessed=blocks * groups * bins * rows * (mics + points) * 2,
            transcendentals=0,
        ),
        name="beams",
    )(spectra, *waves)
    return out.reshape(groups, bins, blocks * rows, points)


def fold_pair(x, bit):
    sectors = lax.axis_size("sector")
    mine = lax.axis_index("sector") // bit % 2
    halves = x.reshape((x.shape[0] // 2, 2) + x.shape[1:])
    sent = lax.dynamic_index_in_dim(halves, 1 - mine, 1, keepdims=False).astype(jnp.bfloat16)
    kept = lax.dynamic_index_in_dim(halves, mine, 1, keepdims=False)
    got = lax.ppermute(sent, "sector", [(i, i ^ bit) for i in range(sectors)])
    return kept.astype(jnp.float32) + got.astype(jnp.float32)


def fold_line(state, stride, step):
    x, right, left = state
    length = x.shape[0]
    place = lax.axis_index("sector") // stride

    def entry(i):
        return lax.dynamic_index_in_dim(x, jnp.clip(i, 0, length - 1), 0, keepdims=False)

    def joined(entry, got):
        return entry if got is None else entry + got.astype(jnp.float32)

    if step == length:
        return joined(joined(entry(place), right), left)
    send_right = joined(entry(length - step + place), right).astype(jnp.bfloat16)
    send_left = joined(entry(place + step - length), left).astype(jnp.bfloat16)
    movers = [i for i in range(length - 1) if i < step]
    pairs = [(i * stride + j, (i + 1) * stride + j) for i in movers for j in range(stride)]
    last = stride * length - 1
    right = lax.ppermute(send_right, "sector", pairs)
    left = lax.ppermute(send_left, "sector", [(last - a, last - b) for a, b in pairs])
    return x, right, left


def fold_stages(sectors):
    stages = []
    stride = 1
    while stride < 4 and sectors // stride % 2 == 0:
        stages.append(functools.partial(fold_pair, bit=stride))
        stride *= 2
    length = sectors // stride
    for step in range(1, length):
        if step == 1:
            stages.append(lambda x: fold_line((x, None, None), stride, 1))
        else:
            stages.append(functools.partial(fold_line, stride=stride, step=step))
    if length > 1:
        final = functools.partial(fold_line, stride=stride, step=length)
    else:
        final = lambda x: x[0]
    return stages, final


def add_over_blk(power):
    devices = lax.axis_size("blk")
    mine = lax.axis_index("blk")
    parts = power.reshape((devices, power.shape[0] // devices) + power.shape[1:])
    total = lax.dynamic_index_in_dim(parts, mine, 0, keepdims=False)
    for shift in range(1, devices):
        sent = lax.dynamic_index_in_dim(parts, (mine + shift) % devices, 0, keepdims=False)
        total += lax.ppermute(sent, "blk", [(i, (i + shift) % devices) for i in range(devices)])
    return total


def local(signal, offsets, fraction, radius, azimuth):
    blocks, mics, length = signal.shape
    sectors = lax.axis_size("sector")
    sector = lax.axis_index("sector")
    total_mics = mics * sectors
    segments = length // HALF - 1
    edge = lax.ppermute(
        signal[:, :1, :], "sector", [(i, (i - 1) % sectors) for i in range(sectors)]
    )
    spectra = spectra_of(signal, edge, fraction[:, None, :], fourier_table())

    band = HALF // sectors
    bins = band // PARTS
    spectra = spectra.reshape(blocks, sectors, PARTS, bins, 2 * ROWS, mics)
    index = (sector * mics + lax.iota(jnp.int32, mics)[None, :] - offsets[:, None]) % total_mics
    phase = wavenumber * distances(index, radius, azimuth, total_mics)
    one = lax.optimization_barrier((jnp.cos(phase), jnp.sin(phase)))

    def joint(a, b):
        return a[0] * b[0] - a[1] * b[1], a[1] * b[0] + a[0] * b[1]

    def power_of(count):
        total, factor = None, one
        while count:
            if count % 2:
                total = factor if total is None else joint(total, factor)
            factor = joint(factor, factor)
            count //= 2
        return total

    step = power_of(band)
    stages, final = fold_stages(sectors)
    states = [None] * PARTS
    for tick in range(PARTS + len(stages)):
        for part in range(PARTS):
            stage = tick - part
            if stage == 0:
                first = power_of(part * bins) if part else ()
                states[part] = beams(spectra, one + step + first, part)
            elif 0 < stage <= len(stages):
                states[part] = stages[stage - 1](states[part])
        states, spectra = lax.optimization_barrier((states, spectra))
    powers = []
    for state in states:
        total = final(state)
        powers.append(jnp.sum(total * total, 1))
    scale = 1.0 / (total_mics * blocks * segments * lax.axis_size("blk"))
    return add_over_blk(jnp.concatenate(powers, 0) * scale)


def solution(mesh):
    return jax.shard_map(
        local,
        mesh=mesh,
        in_specs=(P("blk", "sector", None), P("blk"), P("blk", None), P(), P()),
        out_specs=P(("sector", "blk"), None),
        check_vma=False,
    )
```

```python
import functools
import math

import jax
import jax.numpy as jnp
from jax import lax
from jax.experimental import pallas as pl
from jax.experimental.pallas import tpu as pltpu
from jax.sharding import PartitionSpec as P

NFFT = 1024
HALF = NFFT // 2
ROWS = 16
SPREAD = 24

wavenumber = 2.0
height = 0.5


def cos_of_turns(count):
    quarter = NFFT // 4
    quadrant = (count + quarter // 2) >> (quarter.bit_length() - 1)
    angle = (count - quadrant * quarter).astype(jnp.float32) * (2.0 * math.pi / NFFT)
    square = angle * angle
    sine = 1.0 / math.factorial(9)
    cosine = 1.0 / math.factorial(8) - square * (1.0 / math.factorial(10))
    cosine = 1.0 + square * (
        -1.0 / 2 + square * (1.0 / 24 + square * (-1.0 / 720 + square * cosine))
    )
    sine = angle * (
        1.0
        + square * (-1.0 / 6 + square * (1.0 / 120 + square * (-1.0 / 5040 + square * sine)))
    )
    value = jnp.where(quadrant & 1 == 0, cosine, sine)
    return jnp.where((quadrant + 1) & 2 == 0, value, -value)


def fourier_table():
    row = lax.broadcasted_iota(jnp.int32, (2 * HALF, NFFT), 0)
    sample = lax.broadcasted_iota(jnp.int32, (2 * HALF, NFFT), 1)
    turns = ((row >> 1) * sample + (row & 1) * (NFFT // 4)) & (NFFT - 1)
    window = 0.5 - 0.5 * cos_of_turns(lax.broadcasted_iota(jnp.int32, (1, NFFT), 1))
    window = lax.optimization_barrier(window * (1.0 / math.sqrt(3.0 * NFFT / 8.0)))
    return (cos_of_turns(turns) * window).astype(jnp.bfloat16)


def distances(index, radius, azimuth, total_mics):
    turn = index.astype(jnp.float32) * (2.0 * math.pi / total_mics)
    cycle_cos = jnp.cos(turn)[..., None]
    cycle_sin = jnp.sin(turn)[..., None]
    across = (radius * jnp.cos(azimuth))[None, None, :]
    along = (radius * jnp.sin(azimuth))[None, None, :]
    squared = (
        1.0
        + height * height
        + (radius * radius)[None, None, :]
        - 2.0 * (cycle_cos * across + cycle_sin * along)
    )
    return jnp.sqrt(squared)


def spectra_kernel(segments, signal_ref, edge_ref, weight_ref, table_ref, out_ref, virtual, spread):
    columns = table_ref.shape[0]
    halves, _, lanes = spread.shape
    mics, length = signal_ref.shape[1:]
    chunk = min(256, HALF)

    @pl.when(pl.program_id(1) == 0)
    def _():
        @pl.loop(0, length // chunk)
        def _(place):
            where = pl.ds(pl.multiple_of(place * chunk, chunk), chunk)
            lower = signal_ref[0, :, where].astype(jnp.float32)
            edge = edge_ref[0, :, where].astype(jnp.float32)
            weight = weight_ref[0, :, where]
            row = lax.broadcasted_iota(jnp.int32, lower.shape, 0)
            upper = jnp.where(row == mics - 1, edge, pltpu.roll(lower, mics - 1, 0))
            mixed = (1.0 - weight) * lower + weight * upper
            virtual[where, :] = mixed.T.astype(jnp.bfloat16)

    @pl.loop(0, segments)
    def _(segment):
        start = pl.multiple_of(segment * HALF, HALF)
        product = jnp.dot(
            table_ref[...], virtual[pl.ds(start, NFFT), :], preferred_element_type=jnp.float32
        )
        for half in range(halves):
            spread[half, pl.ds(segment, columns, stride=SPREAD), :] = product[
                :, half * lanes : (half + 1) * lanes
            ]

    for half in range(halves):
        for pad in range(segments, ROWS):
            spread[half, pl.ds(pad, columns, stride=SPREAD), :] = jnp.zeros(
                (columns, lanes), jnp.float32
            )
        rows = spread[half].reshape(columns, SPREAD, lanes)[:, :ROWS]
        out_ref[0, :, half * lanes : (half + 1) * lanes] = rows.reshape(
            columns * ROWS, lanes
        ).astype(jnp.bfloat16)


def spectra_of(signal, edge, weight, table):
    blocks, mics, length = signal.shape
    segments = length // HALF - 1
    tile = HALF
    lanes = min(mics, 128)
    return pl.pallas_call(
        functools.partial(spectra_kernel, segments),
        grid=(blocks, 2 * HALF // tile),
        in_specs=[
            pl.BlockSpec((1, mics, length), lambda b, c: (b, 0, 0)),
            pl.BlockSpec((1, 1, length), lambda b, c: (b, 0, 0)),
            pl.BlockSpec((1, 1, length), lambda b, c: (b, 0, 0)),
            pl.BlockSpec((tile, NFFT), lambda b, c: (c, 0)),
        ],
        out_specs=pl.BlockSpec((1, tile * ROWS, mics), lambda b, c: (b, c, 0)),
        out_shape=jax.ShapeDtypeStruct((blocks, 2 * HALF * ROWS, mics), jnp.bfloat16),
        scratch_shapes=[
            pltpu.VMEM((length, mics), jnp.bfloat16),
            pltpu.VMEM((mics // lanes, tile * SPREAD, lanes), jnp.float32),
        ],
        compiler_params=pltpu.CompilerParams(vmem_limit_bytes=50 << 20),
        name="welch",
    )(signal, edge, weight, table)


def beam_kernel(*refs):
    spectra_ref, one_cos, one_sin, step_cos, step_sin, *firsts = refs[:-4]
    out_ref, now, even, odd = refs[-4:]
    blocks, groups, _, bins = spectra_ref.shape[:4]
    mics = one_cos.shape[1]
    units = blocks * groups

    def generate(unit, steer):
        block = unit // groups
        for tile in range(mics // ROWS):
            rows = pl.ds(tile * ROWS, ROWS)
            cos0, sin0 = now[0, rows], now[1, rows]
            cos1, sin1 = one_cos[block, rows], one_sin[block, rows]
            next_cos = cos0 * cos1 - sin0 * sin1
            next_sin = sin0 * cos1 + cos0 * sin1
            double = cos1 + cos1
            turn_cos, turn_sin = step_cos[block, rows], step_sin[block, rows]
            now[0, rows] = cos0 * turn_cos - sin0 * turn_sin
            now[1, rows] = sin0 * turn_cos + cos0 * turn_sin
            for place in range(bins):
                steer[place, 0, rows] = cos0.astype(jnp.bfloat16)
                steer[place, 1, rows] = sin0.astype(jnp.bfloat16)
                cos0, next_cos = next_cos, double * next_cos - cos0
                sin0, next_sin = next_sin, double * next_sin - sin0

    def multiply(unit, steer):
        block, group = unit // groups, unit % groups
        for place in range(bins):
            rows = spectra_ref[block, group, 0, place]
            turned = jnp.concatenate([rows[ROWS:], -rows[:ROWS]], 0)
            product = jnp.dot(rows, steer[place, 0], preferred_element_type=jnp.float32)
            product += jnp.dot(turned, steer[place, 1], preferred_element_type=jnp.float32)
            out_ref[group, place, block] = product.astype(jnp.bfloat16)

    @pl.loop(0, units // 2)
    def _(pair):
        @pl.when(2 * pair % groups == 0)
        def _():
            if firsts:
                now[0] = firsts[0][2 * pair // groups]
                now[1] = firsts[1][2 * pair // groups]
            else:
                now[0] = jnp.ones(now.shape[1:], jnp.float32)
                now[1] = jnp.zeros(now.shape[1:], jnp.float32)

        multiply(jnp.maximum(2 * pair - 1, 0), odd)
        generate(2 * pair, even)
        multiply(2 * pair, even)
        generate(2 * pair + 1, odd)

    multiply(units - 1, odd)


def beams(spectra, waves, part):
    blocks, groups, _, bins, rows, mics = spectra.shape
    points = waves[0].shape[-1]
    wave = pl.BlockSpec((blocks, mics, points), lambda i: (0, 0, 0))
    out = pl.pallas_call(
        beam_kernel,
        grid=(1,),
        in_specs=[
            pl.BlockSpec((blocks, groups, 1, bins, rows, mics), lambda i: (0, 0, part, 0, 0, 0))
        ]
        + [wave] * len(waves),
        out_specs=pl.BlockSpec((groups, bins, blocks, rows, points), lambda i: (0, 0, 0, 0, 0)),
        out_shape=jax.ShapeDtypeStruct((groups, bins, blocks, rows, points), jnp.bfloat16),
        scratch_shapes=[
            pltpu.VMEM((2, mics, points), jnp.float32),
            pltpu.VMEM((bins, 2, mics, points), jnp.bfloat16),
            pltpu.VMEM((bins, 2, mics, points), jnp.bfloat16),
        ],
        compiler_params=pltpu.CompilerParams(vmem_limit_bytes=48 << 20),
        cost_estimate=pl.CostEstimate(
            flops=32 * blocks * groups * bins * rows * mics * points,
            bytes_accessed=blocks * groups * bins * rows * (mics + points) * 2,
            transcendentals=0,
        ),
        name="beams",
    )(spectra, *waves)
    return out.reshape(groups, bins, blocks * rows, points)


def fold_pair(x, bit):
    sectors = lax.axis_size("sector")
    mine = lax.axis_index("sector") // bit % 2
    halves = x.reshape((x.shape[0] // 2, 2) + x.shape[1:])
    sent = lax.dynamic_index_in_dim(halves, 1 - mine, 1, keepdims=False).astype(jnp.bfloat16)
    kept = lax.dynamic_index_in_dim(halves, mine, 1, keepdims=False)
    got = lax.ppermute(sent, "sector", [(i, i ^ bit) for i in range(sectors)])
    return kept.astype(jnp.float32) + got.astype(jnp.float32)


def fold_line(x, stride):
    length = x.shape[0]
    place = lax.axis_index("sector") // stride
    total = lax.dynamic_index_in_dim(x, place, 0, keepdims=False)
    devices = stride * length
    for shift in range(1, length):
        target = (place + shift) % length
        sent = lax.dynamic_index_in_dim(x, target, 0, keepdims=False).astype(jnp.bfloat16)
        pairs = [(i, (i + shift * stride) % devices) for i in range(devices)]
        total += lax.ppermute(sent, "sector", pairs).astype(jnp.float32)
    return total


def fold_stages(sectors):
    stages = []
    stride = 1
    while stride < 4 and sectors // stride % 2 == 0:
        stages.append(functools.partial(fold_pair, bit=stride))
        stride *= 2
    stages.append(functools.partial(fold_line, stride=stride))
    return stages


def bin_chunks(band):
    if band % 8:
        return [1] * band
    return [band // 4] * 3 + [band // 8] * 2


def add_over_blk(power):
    devices = lax.axis_size("blk")
    mine = lax.axis_index("blk")
    parts = power.reshape((devices, power.shape[0] // devices) + power.shape[1:])
    total = lax.dynamic_index_in_dim(parts, mine, 0, keepdims=False)
    for shift in range(1, devices):
        sent = lax.dynamic_index_in_dim(parts, (mine + shift) % devices, 0, keepdims=False)
        total += lax.ppermute(sent, "blk", [(i, (i + shift) % devices) for i in range(devices)])
    return total


def local(signal, offsets, fraction, radius, azimuth):
    blocks, mics, length = signal.shape
    sectors = lax.axis_size("sector")
    sector = lax.axis_index("sector")
    total_mics = mics * sectors
    segments = length // HALF - 1
    edge = lax.ppermute(
        signal[:, :1, :], "sector", [(i, (i - 1) % sectors) for i in range(sectors)]
    )
    spectra = spectra_of(signal, edge, fraction[:, None, :], fourier_table())

    band = HALF // sectors
    index = (sector * mics + lax.iota(jnp.int32, mics)[None, :] - offsets[:, None]) % total_mics
    phase = wavenumber * distances(index, radius, azimuth, total_mics)
    one = lax.optimization_barrier((jnp.cos(phase), jnp.sin(phase)))

    def joint(a, b):
        return a[0] * b[0] - a[1] * b[1], a[1] * b[0] + a[0] * b[1]

    def power_of(count):
        total, factor = None, one
        while count:
            if count % 2:
                total = factor if total is None else joint(total, factor)
            factor = joint(factor, factor)
            count //= 2
        return total

    step = power_of(band)
    stages = fold_stages(sectors)
    chunks = bin_chunks(band)
    states = [None] * len(chunks)
    for tick in range(len(chunks) + len(stages)):
        for part, bins in enumerate(chunks):
            stage = tick - part
            if stage == 0:
                start = sum(chunks[:part])
                first = power_of(start) if start else ()
                shaped = spectra.reshape(blocks, sectors, band // bins, bins, 2 * ROWS, mics)
                states[part] = beams(shaped, one + step + first, start // bins)
            elif 0 < stage <= len(stages):
                states[part] = stages[stage - 1](states[part])
        states, spectra = lax.optimization_barrier((states, spectra))
    powers = [jnp.sum(total * total, 1) for total in states]
    scale = 1.0 / (total_mics * blocks * segments * lax.axis_size("blk"))
    return add_over_blk(jnp.concatenate(powers, 0) * scale)


def solution(mesh):
    return jax.shard_map(
        local,
        mesh=mesh,
        in_specs=(P("blk", "sector", None), P("blk"), P("blk", None), P(), P()),
        out_specs=P(("sector", "blk"), None),
        check_vma=False,
    )
```

```python
import functools
import math

import jax
import jax.numpy as jnp
from jax import lax
from jax.experimental import pallas as pl
from jax.experimental.pallas import tpu as pltpu
from jax.sharding import PartitionSpec as P

NFFT = 1024
HALF = NFFT // 2
ROWS = 16
SPREAD = 24

wavenumber = 2.0
height = 0.5


def cos_of_turns(count):
    quarter = NFFT // 4
    quadrant = (count + quarter // 2) >> (quarter.bit_length() - 1)
    angle = (count - quadrant * quarter).astype(jnp.float32) * (2.0 * math.pi / NFFT)
    square = angle * angle
    sine = 1.0 / math.factorial(9)
    cosine = 1.0 / math.factorial(8) - square * (1.0 / math.factorial(10))
    cosine = 1.0 + square * (
        -1.0 / 2 + square * (1.0 / 24 + square * (-1.0 / 720 + square * cosine))
    )
    sine = angle * (
        1.0
        + square * (-1.0 / 6 + square * (1.0 / 120 + square * (-1.0 / 5040 + square * sine)))
    )
    value = jnp.where(quadrant & 1 == 0, cosine, sine)
    return jnp.where((quadrant + 1) & 2 == 0, value, -value)


def fourier_table():
    row = lax.broadcasted_iota(jnp.int32, (2 * HALF, NFFT), 0)
    sample = lax.broadcasted_iota(jnp.int32, (2 * HALF, NFFT), 1)
    turns = ((row >> 1) * sample + (row & 1) * (NFFT // 4)) & (NFFT - 1)
    window = 0.5 - 0.5 * cos_of_turns(lax.broadcasted_iota(jnp.int32, (1, NFFT), 1))
    window = lax.optimization_barrier(window * (1.0 / math.sqrt(3.0 * NFFT / 8.0)))
    return (cos_of_turns(turns) * window).astype(jnp.bfloat16)


def distances(index, radius, azimuth, total_mics):
    turn = index.astype(jnp.float32) * (2.0 * math.pi / total_mics)
    cycle_cos = jnp.cos(turn)[..., None]
    cycle_sin = jnp.sin(turn)[..., None]
    across = (radius * jnp.cos(azimuth))[None, None, :]
    along = (radius * jnp.sin(azimuth))[None, None, :]
    squared = (
        1.0
        + height * height
        + (radius * radius)[None, None, :]
        - 2.0 * (cycle_cos * across + cycle_sin * along)
    )
    return jnp.sqrt(squared)


def spectra_kernel(segments, signal_ref, edge_ref, weight_ref, table_ref, out_ref, virtual, spread):
    columns = table_ref.shape[0]
    halves, _, lanes = spread.shape
    mics, length = signal_ref.shape[1:]
    chunk = min(256, HALF)

    @pl.when(pl.program_id(1) == 0)
    def _():
        @pl.loop(0, length // chunk)
        def _(place):
            where = pl.ds(pl.multiple_of(place * chunk, chunk), chunk)
            lower = signal_ref[0, :, where].astype(jnp.float32)
            edge = edge_ref[0, :, where].astype(jnp.float32)
            weight = weight_ref[0, :, where]
            row = lax.broadcasted_iota(jnp.int32, lower.shape, 0)
            upper = jnp.where(row == mics - 1, edge, pltpu.roll(lower, mics - 1, 0))
            mixed = (1.0 - weight) * lower + weight * upper
            virtual[where, :] = mixed.T.astype(jnp.bfloat16)

    @pl.loop(0, segments, unroll=3 if segments % 3 == 0 else 1)
    def _(segment):
        start = pl.multiple_of(segment * HALF, HALF)
        product = jnp.dot(
            table_ref[...], virtual[pl.ds(start, NFFT), :], preferred_element_type=jnp.float32
        )
        for half in range(halves):
            spread[half, pl.ds(segment, columns, stride=SPREAD), :] = product[
                :, half * lanes : (half + 1) * lanes
            ]

    for half in range(halves):
        for pad in range(segments, ROWS):
            spread[half, pl.ds(pad, columns, stride=SPREAD), :] = jnp.zeros(
                (columns, lanes), jnp.float32
            )
        rows = spread[half].reshape(columns, SPREAD, lanes)[:, :ROWS]
        out_ref[0, :, half * lanes : (half + 1) * lanes] = rows.reshape(
            columns * ROWS, lanes
        ).astype(jnp.bfloat16)


def spectra_of(signal, edge, weight, table):
    blocks, mics, length = signal.shape
    segments = length // HALF - 1
    tile = HALF
    lanes = min(mics, 128)
    return pl.pallas_call(
        functools.partial(spectra_kernel, segments),
        grid=(blocks, 2 * HALF // tile),
        in_specs=[
            pl.BlockSpec((1, mics, length), lambda b, c: (b, 0, 0)),
            pl.BlockSpec((1, 1, length), lambda b, c: (b, 0, 0)),
            pl.BlockSpec((1, 1, length), lambda b, c: (b, 0, 0)),
            pl.BlockSpec((tile, NFFT), lambda b, c: (c, 0)),
        ],
        out_specs=pl.BlockSpec((1, tile * ROWS, mics), lambda b, c: (b, c, 0)),
        out_shape=jax.ShapeDtypeStruct((blocks, 2 * HALF * ROWS, mics), jnp.bfloat16),
        scratch_shapes=[
            pltpu.VMEM((length, mics), jnp.bfloat16),
            pltpu.VMEM((mics // lanes, tile * SPREAD, lanes), jnp.float32),
        ],
        compiler_params=pltpu.CompilerParams(vmem_limit_bytes=50 << 20),
        name="welch",
    )(signal, edge, weight, table)


def beam_kernel(*refs):
    spectra_ref, one_cos, one_sin, step_cos, step_sin, *firsts = refs[:-4]
    out_ref, now, even, odd = refs[-4:]
    blocks, groups, _, bins = spectra_ref.shape[:4]
    mics = one_cos.shape[1]
    units = blocks * groups

    def generate(unit, steer, tile):
        block = unit // groups
        rows = pl.ds(tile * ROWS, ROWS)
        sin_rows = pl.ds(mics + tile * ROWS, ROWS)
        cos0, sin0 = now[0, rows], now[1, rows]
        cos1, sin1 = one_cos[block, rows], one_sin[block, rows]
        next_cos = cos0 * cos1 - sin0 * sin1
        next_sin = sin0 * cos1 + cos0 * sin1
        double = cos1 + cos1
        turn_cos, turn_sin = step_cos[block, rows], step_sin[block, rows]
        now[0, rows] = cos0 * turn_cos - sin0 * turn_sin
        now[1, rows] = sin0 * turn_cos + cos0 * turn_sin
        for place in range(bins):
            steer[place, rows] = cos0.astype(jnp.bfloat16)
            steer[place, sin_rows] = sin0.astype(jnp.bfloat16)
            cos0, next_cos = next_cos, double * next_cos - cos0
            sin0, next_sin = next_sin, double * next_sin - sin0

    def multiply(unit, steer, place):
        block, group = unit // groups, unit % groups
        rows = spectra_ref[block, group, 0, place]
        turned = jnp.concatenate([rows[ROWS:], -rows[:ROWS]], 0)
        if mics % 128 == 0:
            both = jnp.concatenate([rows, turned], 1)
            product = jnp.dot(both, steer[place], preferred_element_type=jnp.float32)
        else:
            product = jnp.dot(rows, steer[place, :mics], preferred_element_type=jnp.float32)
            product += jnp.dot(turned, steer[place, mics:], preferred_element_type=jnp.float32)
        out_ref[group, place, block] = product.astype(jnp.bfloat16)

    def both(made, steer, used, other):
        tiles = mics // ROWS
        for tile in range(tiles):
            for place in range(tile * bins // tiles, (tile + 1) * bins // tiles):
                multiply(used, other, place)
            generate(made, steer, tile)

    @pl.loop(0, units // 2)
    def _(pair):
        @pl.when(2 * pair % groups == 0)
        def _():
            if firsts:
                now[0] = firsts[0][2 * pair // groups]
                now[1] = firsts[1][2 * pair // groups]
            else:
                now[0] = jnp.ones(now.shape[1:], jnp.float32)
                now[1] = jnp.zeros(now.shape[1:], jnp.float32)

        both(2 * pair, even, jnp.maximum(2 * pair - 1, 0), odd)
        both(2 * pair + 1, odd, 2 * pair, even)

    for place in range(bins):
        multiply(units - 1, odd, place)


def beams(spectra, waves, part):
    blocks, groups, _, bins, rows, mics = spectra.shape
    points = waves[0].shape[-1]
    wave = pl.BlockSpec((blocks, mics, points), lambda i: (0, 0, 0))
    out = pl.pallas_call(
        beam_kernel,
        grid=(1,),
        in_specs=[
            pl.BlockSpec((blocks, groups, 1, bins, rows, mics), lambda i: (0, 0, part, 0, 0, 0))
        ]
        + [wave] * len(waves),
        out_specs=pl.BlockSpec((groups, bins, blocks, rows, points), lambda i: (0, 0, 0, 0, 0)),
        out_shape=jax.ShapeDtypeStruct((groups, bins, blocks, rows, points), jnp.bfloat16),
        scratch_shapes=[
            pltpu.VMEM((2, mics, points), jnp.float32),
            pltpu.VMEM((bins, 2 * mics, points), jnp.bfloat16),
            pltpu.VMEM((bins, 2 * mics, points), jnp.bfloat16),
        ],
        compiler_params=pltpu.CompilerParams(vmem_limit_bytes=48 << 20),
        cost_estimate=pl.CostEstimate(
            flops=32 * blocks * groups * bins * rows * mics * points,
            bytes_accessed=blocks * groups * bins * rows * (mics + points) * 2,
            transcendentals=0,
        ),
        name="beams",
    )(spectra, *waves)
    return out.reshape(groups, bins, blocks * rows, points)


def fold_pair(x, bit, kind):
    sectors = lax.axis_size("sector")
    mine = lax.axis_index("sector") // bit % 2
    halves = x.reshape((x.shape[0] // 2, 2) + x.shape[1:])
    sent = lax.dynamic_index_in_dim(halves, 1 - mine, 1, keepdims=False).astype(jnp.bfloat16)
    kept = lax.dynamic_index_in_dim(halves, mine, 1, keepdims=False)
    got = lax.ppermute(sent, "sector", [(i, i ^ bit) for i in range(sectors)])
    return (kept.astype(jnp.float32) + got.astype(jnp.float32)).astype(kind)


def fold_line(x, stride):
    length = x.shape[0]
    place = lax.axis_index("sector") // stride
    total = lax.dynamic_index_in_dim(x, place, 0, keepdims=False).astype(jnp.float32)
    devices = stride * length
    for shift in range(1, length):
        target = (place + shift) % length
        sent = lax.dynamic_index_in_dim(x, target, 0, keepdims=False).astype(jnp.bfloat16)
        pairs = [(i, (i + shift * stride) % devices) for i in range(devices)]
        total += lax.ppermute(sent, "sector", pairs).astype(jnp.float32)
    return total


def fold_stages(sectors):
    stages = []
    stride = 1
    while stride < 4 and sectors // stride % 2 == 0:
        kind = jnp.bfloat16 if stride == 1 else jnp.float32
        stages.append(functools.partial(fold_pair, bit=stride, kind=kind))
        stride *= 2
    stages.append(functools.partial(fold_line, stride=stride))
    return stages


def bin_chunks(band):
    if band % 8:
        return [1] * band
    return [band // 4] * 3 + [band // 8] * 2


def add_over_blk(power):
    devices = lax.axis_size("blk")
    mine = lax.axis_index("blk")
    parts = power.reshape((devices, power.shape[0] // devices) + power.shape[1:])
    total = lax.dynamic_index_in_dim(parts, mine, 0, keepdims=False)
    for shift in range(1, devices):
        sent = lax.dynamic_index_in_dim(parts, (mine + shift) % devices, 0, keepdims=False)
        total += lax.ppermute(sent, "blk", [(i, (i + shift) % devices) for i in range(devices)])
    return total


def local(signal, offsets, fraction, radius, azimuth):
    blocks, mics, length = signal.shape
    sectors = lax.axis_size("sector")
    sector = lax.axis_index("sector")
    total_mics = mics * sectors
    segments = length // HALF - 1
    edge = lax.ppermute(
        signal[:, :1, :], "sector", [(i, (i - 1) % sectors) for i in range(sectors)]
    )
    spectra = spectra_of(signal, edge, fraction[:, None, :], fourier_table())

    band = HALF // sectors
    index = (sector * mics + lax.iota(jnp.int32, mics)[None, :] - offsets[:, None]) % total_mics
    phase = wavenumber * distances(index, radius, azimuth, total_mics)
    one = lax.optimization_barrier((jnp.cos(phase), jnp.sin(phase)))

    def joint(a, b):
        return a[0] * b[0] - a[1] * b[1], a[1] * b[0] + a[0] * b[1]

    def power_of(count):
        total, factor = None, one
        while count:
            if count % 2:
                total = factor if total is None else joint(total, factor)
            factor = joint(factor, factor)
            count //= 2
        return total

    step = power_of(band)
    stages = fold_stages(sectors)
    chunks = bin_chunks(band)
    states = [None] * len(chunks)
    for tick in range(len(chunks) + len(stages)):
        for part, bins in enumerate(chunks):
            stage = tick - part
            if stage == 0:
                start = sum(chunks[:part])
                first = power_of(start) if start else ()
                shaped = spectra.reshape(blocks, sectors, band // bins, bins, 2 * ROWS, mics)
                states[part] = beams(shaped, one + step + first, start // bins)
            elif 0 < stage <= len(stages):
                states[part] = stages[stage - 1](states[part])
        states, spectra = lax.optimization_barrier((states, spectra))
    powers = [jnp.sum(total * total, 1) for total in states]
    scale = 1.0 / (total_mics * blocks * segments * lax.axis_size("blk"))
    return add_over_blk(jnp.concatenate(powers, 0) * scale)


def solution(mesh):
    return jax.shard_map(
        local,
        mesh=mesh,
        in_specs=(P("blk", "sector", None), P("blk"), P("blk", None), P(), P()),
        out_specs=P(("sector", "blk"), None),
        check_vma=False,
    )
```

```python
import functools
import math

import jax
import jax.numpy as jnp
from jax import lax
from jax.experimental import pallas as pl
from jax.experimental.pallas import tpu as pltpu
from jax.sharding import PartitionSpec as P

NFFT = 1024
HALF = NFFT // 2
ROWS = 16
SPREAD = 24

wavenumber = 2.0
height = 0.5


def cos_of_turns(count):
    quarter = NFFT // 4
    quadrant = (count + quarter // 2) >> (quarter.bit_length() - 1)
    angle = (count - quadrant * quarter).astype(jnp.float32) * (2.0 * math.pi / NFFT)
    square = angle * angle
    sine = 1.0 / math.factorial(9)
    cosine = 1.0 / math.factorial(8) - square * (1.0 / math.factorial(10))
    cosine = 1.0 + square * (
        -1.0 / 2 + square * (1.0 / 24 + square * (-1.0 / 720 + square * cosine))
    )
    sine = angle * (
        1.0
        + square * (-1.0 / 6 + square * (1.0 / 120 + square * (-1.0 / 5040 + square * sine)))
    )
    value = jnp.where(quadrant & 1 == 0, cosine, sine)
    return jnp.where((quadrant + 1) & 2 == 0, value, -value)


def fourier_table():
    row = lax.broadcasted_iota(jnp.int32, (2 * HALF, NFFT), 0)
    sample = lax.broadcasted_iota(jnp.int32, (2 * HALF, NFFT), 1)
    turns = ((row >> 1) * sample + (row & 1) * (NFFT // 4)) & (NFFT - 1)
    window = 0.5 - 0.5 * cos_of_turns(lax.broadcasted_iota(jnp.int32, (1, NFFT), 1))
    window = lax.optimization_barrier(window * (1.0 / math.sqrt(3.0 * NFFT / 8.0)))
    return (cos_of_turns(turns) * window).astype(jnp.bfloat16)


def distances(index, radius, azimuth, total_mics):
    turn = index.astype(jnp.float32) * (2.0 * math.pi / total_mics)
    cycle_cos = jnp.cos(turn)[..., None]
    cycle_sin = jnp.sin(turn)[..., None]
    across = (radius * jnp.cos(azimuth))[None, None, :]
    along = (radius * jnp.sin(azimuth))[None, None, :]
    squared = (
        1.0
        + height * height
        + (radius * radius)[None, None, :]
        - 2.0 * (cycle_cos * across + cycle_sin * along)
    )
    return jnp.sqrt(squared)


def spectra_kernel(segments, signal_ref, edge_ref, weight_ref, table_ref, out_ref, virtual, spread):
    columns = table_ref.shape[0]
    halves, _, lanes = spread.shape
    mics, length = signal_ref.shape[1:]
    chunk = min(256, HALF)

    @pl.when(pl.program_id(1) == 0)
    def _():
        @pl.loop(0, length // chunk)
        def _(place):
            where = pl.ds(pl.multiple_of(place * chunk, chunk), chunk)
            lower = signal_ref[0, :, where].astype(jnp.float32)
            edge = edge_ref[0, :, where].astype(jnp.float32)
            weight = weight_ref[0, :, where]
            row = lax.broadcasted_iota(jnp.int32, lower.shape, 0)
            upper = jnp.where(row == mics - 1, edge, pltpu.roll(lower, mics - 1, 0))
            mixed = (1.0 - weight) * lower + weight * upper
            virtual[where, :] = mixed.T.astype(jnp.bfloat16)

    @pl.loop(0, segments, unroll=3 if segments % 3 == 0 else 1)
    def _(segment):
        start = pl.multiple_of(segment * HALF, HALF)
        product = jnp.dot(
            table_ref[...], virtual[pl.ds(start, NFFT), :], preferred_element_type=jnp.float32
        )
        for half in range(halves):
            spread[half, pl.ds(segment, columns, stride=SPREAD), :] = product[
                :, half * lanes : (half + 1) * lanes
            ]

    for half in range(halves):
        for pad in range(segments, ROWS):
            spread[half, pl.ds(pad, columns, stride=SPREAD), :] = jnp.zeros(
                (columns, lanes), jnp.float32
            )
        rows = spread[half].reshape(columns, SPREAD, lanes)[:, :ROWS]
        out_ref[0, :, half * lanes : (half + 1) * lanes] = rows.reshape(
            columns * ROWS, lanes
        ).astype(jnp.bfloat16)


def spectra_of(signal, edge, weight, table):
    blocks, mics, length = signal.shape
    segments = length // HALF - 1
    tile = HALF
    lanes = min(mics, 128)
    return pl.pallas_call(
        functools.partial(spectra_kernel, segments),
        grid=(blocks, 2 * HALF // tile),
        in_specs=[
            pl.BlockSpec((1, mics, length), lambda b, c: (b, 0, 0)),
            pl.BlockSpec((1, 1, length), lambda b, c: (b, 0, 0)),
            pl.BlockSpec((1, 1, length), lambda b, c: (b, 0, 0)),
            pl.BlockSpec((tile, NFFT), lambda b, c: (c, 0)),
        ],
        out_specs=pl.BlockSpec((1, tile * ROWS, mics), lambda b, c: (b, c, 0)),
        out_shape=jax.ShapeDtypeStruct((blocks, 2 * HALF * ROWS, mics), jnp.bfloat16),
        scratch_shapes=[
            pltpu.VMEM((length, mics), jnp.bfloat16),
            pltpu.VMEM((mics // lanes, tile * SPREAD, lanes), jnp.float32),
        ],
        compiler_params=pltpu.CompilerParams(vmem_limit_bytes=50 << 20),
        name="welch",
    )(signal, edge, weight, table)


def beam_kernel(*refs):
    spectra_ref, one_cos, one_sin, step_cos, step_sin, *firsts = refs[:-4]
    out_ref, now, even, odd = refs[-4:]
    blocks, groups, _, bins = spectra_ref.shape[:4]
    mics = one_cos.shape[1]
    units = blocks * groups

    def generate(unit, steer, tile):
        block = unit // groups
        rows = pl.ds(tile * ROWS, ROWS)
        sin_rows = pl.ds(mics + tile * ROWS, ROWS)
        cos0, sin0 = now[0, rows], now[1, rows]
        cos1, sin1 = one_cos[block, rows], one_sin[block, rows]
        next_cos = cos0 * cos1 - sin0 * sin1
        next_sin = sin0 * cos1 + cos0 * sin1
        double = cos1 + cos1
        turn_cos, turn_sin = step_cos[block, rows], step_sin[block, rows]
        now[0, rows] = cos0 * turn_cos - sin0 * turn_sin
        now[1, rows] = sin0 * turn_cos + cos0 * turn_sin
        for place in range(bins):
            steer[place, rows] = cos0.astype(jnp.bfloat16)
            steer[place, sin_rows] = sin0.astype(jnp.bfloat16)
            cos0, next_cos = next_cos, double * next_cos - cos0
            sin0, next_sin = next_sin, double * next_sin - sin0

    def multiply(unit, steer, place):
        block, group = unit // groups, unit % groups
        rows = spectra_ref[block, group, 0, place]
        turned = jnp.concatenate([rows[ROWS:], -rows[:ROWS]], 0)
        product = jnp.dot(rows, steer[place, :mics], preferred_element_type=jnp.float32)
        product += jnp.dot(turned, steer[place, mics:], preferred_element_type=jnp.float32)
        out_ref[group, place, block] = product.astype(jnp.bfloat16)

    def both(made, steer, used, other):
        for place in range(bins):
            multiply(used, other, place)
        for tile in range(mics // ROWS):
            generate(made, steer, tile)

    @pl.loop(0, units // 2)
    def _(pair):
        @pl.when(2 * pair % groups == 0)
        def _():
            if firsts:
                now[0] = firsts[0][2 * pair // groups]
                now[1] = firsts[1][2 * pair // groups]
            else:
                now[0] = jnp.ones(now.shape[1:], jnp.float32)
                now[1] = jnp.zeros(now.shape[1:], jnp.float32)

        both(2 * pair, even, jnp.maximum(2 * pair - 1, 0), odd)
        both(2 * pair + 1, odd, 2 * pair, even)

    for place in range(bins):
        multiply(units - 1, odd, place)


def beams(spectra, waves, part):
    blocks, groups, _, bins, rows, mics = spectra.shape
    points = waves[0].shape[-1]
    wave = pl.BlockSpec((blocks, mics, points), lambda i: (0, 0, 0))
    out = pl.pallas_call(
        beam_kernel,
        grid=(1,),
        in_specs=[
            pl.BlockSpec((blocks, groups, 1, bins, rows, mics), lambda i: (0, 0, part, 0, 0, 0))
        ]
        + [wave] * len(waves),
        out_specs=pl.BlockSpec((groups, bins, blocks, rows, points), lambda i: (0, 0, 0, 0, 0)),
        out_shape=jax.ShapeDtypeStruct((groups, bins, blocks, rows, points), jnp.bfloat16),
        scratch_shapes=[
            pltpu.VMEM((2, mics, points), jnp.float32),
            pltpu.VMEM((bins, 2 * mics, points), jnp.bfloat16),
            pltpu.VMEM((bins, 2 * mics, points), jnp.bfloat16),
        ],
        compiler_params=pltpu.CompilerParams(vmem_limit_bytes=48 << 20),
        cost_estimate=pl.CostEstimate(
            flops=32 * blocks * groups * bins * rows * mics * points,
            bytes_accessed=blocks * groups * bins * rows * (mics + points) * 2,
            transcendentals=0,
        ),
        name="beams",
    )(spectra, *waves)
    return out.reshape(groups, bins, blocks * rows, points)


def fold_pair(x, bit, kind):
    sectors = lax.axis_size("sector")
    mine = lax.axis_index("sector") // bit % 2
    halves = x.reshape((x.shape[0] // 2, 2) + x.shape[1:])
    sent = lax.dynamic_index_in_dim(halves, 1 - mine, 1, keepdims=False).astype(jnp.bfloat16)
    kept = lax.dynamic_index_in_dim(halves, mine, 1, keepdims=False)
    got = lax.ppermute(sent, "sector", [(i, i ^ bit) for i in range(sectors)])
    return (kept.astype(jnp.float32) + got.astype(jnp.float32)).astype(kind)


def fold_line(x, stride):
    length = x.shape[0]
    place = lax.axis_index("sector") // stride
    total = lax.dynamic_index_in_dim(x, place, 0, keepdims=False).astype(jnp.float32)
    devices = stride * length
    for shift in range(1, length):
        target = (place + shift) % length
        sent = lax.dynamic_index_in_dim(x, target, 0, keepdims=False).astype(jnp.bfloat16)
        pairs = [(i, (i + shift * stride) % devices) for i in range(devices)]
        total += lax.ppermute(sent, "sector", pairs).astype(jnp.float32)
    return total


def fold_stages(sectors):
    stages = []
    stride = 1
    while stride < 4 and sectors // stride % 2 == 0:
        kind = jnp.bfloat16 if stride == 1 else jnp.float32
        stages.append(functools.partial(fold_pair, bit=stride, kind=kind))
        stride *= 2
    stages.append(functools.partial(fold_line, stride=stride))
    return stages


def bin_chunks(band):
    if band % 8:
        return [1] * band
    return [band // 4] * 3 + [band // 8] * 2


def add_over_blk(power):
    devices = lax.axis_size("blk")
    mine = lax.axis_index("blk")
    parts = power.reshape((devices, power.shape[0] // devices) + power.shape[1:])
    total = lax.dynamic_index_in_dim(parts, mine, 0, keepdims=False)
    for shift in range(1, devices):
        sent = lax.dynamic_index_in_dim(parts, (mine + shift) % devices, 0, keepdims=False)
        total += lax.ppermute(sent, "blk", [(i, (i + shift) % devices) for i in range(devices)])
    return total


def local(signal, offsets, fraction, radius, azimuth):
    blocks, mics, length = signal.shape
    sectors = lax.axis_size("sector")
    sector = lax.axis_index("sector")
    total_mics = mics * sectors
    segments = length // HALF - 1
    edge = lax.ppermute(
        signal[:, :1, :], "sector", [(i, (i - 1) % sectors) for i in range(sectors)]
    )
    spectra = spectra_of(signal, edge, fraction[:, None, :], fourier_table())

    band = HALF // sectors
    index = (sector * mics + lax.iota(jnp.int32, mics)[None, :] - offsets[:, None]) % total_mics
    phase = wavenumber * distances(index, radius, azimuth, total_mics)
    one = lax.optimization_barrier((jnp.cos(phase), jnp.sin(phase)))

    def joint(a, b):
        return a[0] * b[0] - a[1] * b[1], a[1] * b[0] + a[0] * b[1]

    def power_of(count):
        total, factor = None, one
        while count:
            if count % 2:
                total = factor if total is None else joint(total, factor)
            factor = joint(factor, factor)
            count //= 2
        return total

    step = power_of(band)
    stages = fold_stages(sectors)
    chunks = bin_chunks(band)
    states = [None] * len(chunks)
    for tick in range(len(chunks) + len(stages)):
        for part, bins in enumerate(chunks):
            stage = tick - part
            if stage == 0:
                start = sum(chunks[:part])
                first = power_of(start) if start else ()
                shaped = spectra.reshape(blocks, sectors, band // bins, bins, 2 * ROWS, mics)
                states[part] = beams(shaped, one + step + first, start // bins)
            elif 0 < stage <= len(stages):
                states[part] = stages[stage - 1](states[part])
        states, spectra = lax.optimization_barrier((states, spectra))
    powers = [jnp.sum(total * total, 1) for total in states]
    scale = 1.0 / (total_mics * blocks * segments * lax.axis_size("blk"))
    return add_over_blk(jnp.concatenate(powers, 0) * scale)


def solution(mesh):
    return jax.shard_map(
        local,
        mesh=mesh,
        in_specs=(P("blk", "sector", None), P("blk"), P("blk", None), P(), P()),
        out_specs=P(("sector", "blk"), None),
        check_vma=False,
    )
```
